32 devices in a mesh: row: 4 (over y, x), col: 8 (over z, core).
Axes of the slice: x: 2, y: 2, z: 4, core: 2. Of those that a mesh axis runs over, the one named last changes fastest.
Arguments:
- left_features: bfloat16 [384, 4096], P(('row', 'col')), may hold values from -6 to 6
- right_features: bfloat16 [384, 4096], P(('row', 'col')), may hold values from -6 to 6
- weight: bfloat16 [1024, 128], replicated, may hold values from -2 to 2
- bias: float32 [128], replicated, may hold values from -3 to 3
- upstream: bfloat16 [384, 384, 128], P('row', 'col'), may hold values from -0.59765625 to 0.59765625
Outputs:
- pair_out: bfloat16 [384, 384, 128], P('row', 'col')
- grad_left: bfloat16 [384, 4096], P(('row', 'col'))
- grad_right: bfloat16 [384, 4096], P(('row', 'col'))
- grad_weight: float32 [1024, 128], replicated
- grad_bias: float32 [128], replicated
The draws below stay inside these ranges and needn't reach their ends.
All inputs are finite; a program needn't handle non-finite values.
Results may differ from the reference program's by a relative error of at most 0.0063.
Values may be sent and summed in bfloat16 or wider, within the bound.
A program may use at most 128 MiB of HBM per device.

```python
import jax
import jax.numpy as jnp
from jax import lax

CH = 32
PAIR = 128
SEQS = 128
RES = 384


def steps_of(key, shape, pieces, least, top_value):
    factor_of, own = 1.0, jax.random.fold_in(key, 6)
    for position, blocks in pieces:
        draws = jnp.exp(jax.random.uniform(jax.random.fold_in(own, position), (blocks,), jnp.float32, least / len(pieces), top_value / len(pieces)))
        factor_of = factor_of * jnp.repeat(draws, shape[position] // blocks).reshape([-1 if axis == position else 1 for axis in range(len(shape))])
    return factor_of


def scatter_about(rng, dims, spread, limit, shards=(), kind=jnp.bfloat16):
    array = spread * jax.random.normal(rng, dims, jnp.float32)
    if shards:
        array = array * steps_of(rng, dims, shards, -0.22, 0.18)
    return jnp.clip(array, -limit, limit).astype(kind)


def setup_inputs(seed: int = 0) -> dict:
    seeds = jax.random.split(jax.random.key(seed), 6)
    return {
        "left_features": scatter_about(seeds[0], (RES, SEQS * CH), 1.0, 6.0, ((0, 32),)),
        "right_features": scatter_about(seeds[1], (RES, SEQS * CH), 1.0, 6.0, ((0, 32),)),
        "weight": scatter_about(seeds[2], (CH * CH, PAIR), (CH * CH // SEQS) ** -0.5, 2.0),
        "bias": scatter_about(seeds[3], (PAIR,), 0.5, 3.0, (), jnp.float32),
        "upstream": scatter_about(seeds[4], (RES, RES, PAIR), 0.1, 0.59765625, ((0, 4), (1, 8))),
    }


block_rows = 16


def outer_product(rows, columns):
    rows3 = rows.astype(jnp.float32).reshape(rows.shape[0], SEQS, CH)
    cols3 = columns.astype(jnp.float32).reshape(columns.shape[0], SEQS, CH)
    product = jnp.einsum("isc,jsd->ijcd", rows3, cols3, precision=lax.Precision.HIGHEST) * (1.0 / SEQS)
    return product.reshape(rows.shape[0] * columns.shape[0], CH * CH).astype(jnp.bfloat16)


def reference(left_features, right_features, weight, bias, upstream):
    blocks = RES // block_rows

    def forward_block(index):
        rows = lax.dynamic_slice_in_dim(left_features, (index * block_rows).astype(jnp.int32), block_rows, 0)
        outer = outer_product(rows, right_features)
        return jnp.dot(outer, weight, preferred_element_type=jnp.float32) + bias

    pre = lax.map(forward_block, jnp.arange(blocks, dtype=jnp.int32)).reshape(RES, RES, PAIR)
    active = jnp.maximum(pre, 0.0)
    squared = active * active
    pair_out = ((squared + squared.transpose(1, 0, 2)) * 0.5).astype(jnp.bfloat16)
    grads = upstream.astype(jnp.float32)
    d_direct = (active * grads).astype(jnp.bfloat16)
    d_mirror = (active * grads.transpose(1, 0, 2)).astype(jnp.bfloat16)
    right3 = right_features.astype(jnp.float32).reshape(RES, SEQS, CH)
    weight_t = weight.T

    def backward_block(carry, index):
        d_right, d_weight, d_bias = carry
        start = (index * block_rows).astype(jnp.int32)
        rows = lax.dynamic_slice_in_dim(left_features, start, block_rows, 0)
        rows3 = rows.astype(jnp.float32).reshape(block_rows, SEQS, CH)
        outer = outer_product(rows, right_features)
        part_direct = lax.dynamic_slice_in_dim(d_direct, start, block_rows, 0).reshape(-1, PAIR)
        part_mirror = lax.dynamic_slice_in_dim(d_mirror, start, block_rows, 0).reshape(-1, PAIR)
        g_direct = jnp.dot(part_direct, weight_t, preferred_element_type=jnp.float32).astype(jnp.bfloat16)
        g_mirror = jnp.dot(part_mirror, weight_t, preferred_element_type=jnp.float32).astype(jnp.bfloat16)
        total = (g_direct.astype(jnp.float32) + g_mirror.astype(jnp.float32)).reshape(block_rows, RES, CH, CH)
        d_left = jnp.einsum("ijcd,jsd->isc", total, right3, precision=lax.Precision.HIGHEST) * (1.0 / SEQS)
        d_right = d_right + jnp.einsum("ijcd,isc->jsd", total, rows3, precision=lax.Precision.HIGHEST) * (1.0 / SEQS)
        d_weight = d_weight + jnp.dot(outer.T, part_direct, preferred_element_type=jnp.float32)
        d_weight = d_weight + jnp.dot(outer.T, part_mirror, preferred_element_type=jnp.float32)
        d_bias = d_bias + jnp.sum(part_direct.astype(jnp.float32), axis=0) + jnp.sum(part_mirror.astype(jnp.float32), axis=0)
        return (d_right, d_weight, d_bias), d_left.reshape(block_rows, SEQS * CH)

    init = (jnp.zeros((RES, SEQS, CH), jnp.float32), jnp.zeros((CH * CH, PAIR), jnp.float32), jnp.zeros((PAIR,), jnp.float32))
    (d_right, d_weight, d_bias), d_left = lax.scan(backward_block, init, jnp.arange(blocks, dtype=jnp.int32))
    grad_left = d_left.reshape(RES, SEQS * CH).astype(jnp.bfloat16)
    grad_right = d_right.reshape(RES, SEQS * CH).astype(jnp.bfloat16)
    return pair_out, grad_left, grad_right, d_weight, d_bias
```

```python
import functools

import jax
import jax.numpy as jnp
from jax import lax
from jax.experimental import pallas as pl
from jax.experimental.pallas import tpu as pltpu
from jax.sharding import PartitionSpec as P

CH = 32
SEQS = 128
LANES = 128
F32 = jnp.float32
BF16 = jnp.bfloat16


def mm(a, b):
    return lax.dot_general(a, b, (((1,), (0,)), ((), ())), preferred_element_type=F32)


def mm_nt(a, b):
    return lax.dot_general(a, b, (((1,), (1,)), ((), ())), preferred_element_type=F32)


def tile_kernel(
    jb, ni, nj,
    rows_ref, cols_ref, wd_ref, wm_ref, wdt_ref, wmt_ref, bias_ref, up_ref,
    pair_ref, drows_ref, dcols_ref, dw_ref,
    rt, rx, bt, wide, x, gx, d, sq, u32, ut, drt, dw_m, dct, btt,
):
    step = pl.program_id(0)
    last = pl.num_programs(0) - 1
    pairs = wd_ref.shape[1]
    cc = CH * CH
    scale = 1.0 / SEQS
    ndev, _, part, _ = rows_ref.shape
    nparts = cols_ref.shape[0]
    pad = LANES - ni

    @pl.when(step == 0)
    def _():
        for side in range(2):
            for k in range(ndev):
                wide[pl.ds(k * part, part), :] = rows_ref[k, side].astype(F32)
            for k in range(nparts):
                bt[side, pl.ds(k * part, part), :] = cols_ref[k, side]

            def prep(c, _):
                block = wide[pl.ds(c, ni, stride=CH), :]
                if pad:
                    block = jnp.concatenate([block, jnp.zeros((pad, SEQS), F32)], axis=0)
                at = pl.multiple_of(c * LANES, LANES)
                rx[side, pl.ds(at, LANES), :] = block.astype(BF16)
                rt[side, :, pl.ds(at, LANES)] = block.T.astype(BF16)
                return 0

            lax.fori_loop(0, CH, prep, 0)
        drt[...] = jnp.zeros_like(drt)
        dw_ref[...] = jnp.zeros_like(dw_ref)
        dw_m[...] = jnp.zeros_like(dw_m)

    u32[...] = up_ref[...].astype(F32).reshape(ni * jb, pairs)
    for j in range(jb):
        block = u32[pl.ds(j, ni, stride=jb), :]
        if pad:
            block = jnp.concatenate([block, jnp.zeros((pad, pairs), F32)], axis=0)
        ut[:, j * LANES : (j + 1) * LANES] = block.T

    for side in range(2):
        w_ref, wt_ref = (wd_ref, wdt_ref) if side == 0 else (wm_ref, wmt_ref)
        base = pl.multiple_of(step * (jb * CH), jb * CH)
        bt_blk = bt[1 - side, pl.ds(base, jb * CH), :]
        btt[...] = bt_blk.astype(F32).T.astype(BF16)

        def first(cp, _):
            at = pl.multiple_of(cp * 2 * LANES, 2 * LANES)
            r = mm(bt[1 - side, pl.ds(base, jb * CH), :], rt[side, :, pl.ds(at, 2 * LANES)])
            r = (r * scale).astype(BF16)
            for c2 in range(2):
                to = pl.multiple_of(cp * 2 * CH + c2 * CH, CH)
                for j in range(jb):
                    x[pl.ds(to, CH), j * LANES : (j + 1) * LANES] = r[
                        j * CH : (j + 1) * CH, c2 * LANES : (c2 + 1) * LANES
                    ]
            return 0

        lax.fori_loop(0, CH // 2, first, 0)

        def second(jp, _):
            at = pl.multiple_of(jp * 2 * LANES, 2 * LANES)
            pre = mm(wt_ref[...], x[:, pl.ds(at, 2 * LANES)]) + bias_ref[...]
            active = jnp.maximum(pre, 0.0)
            d[:, pl.ds(at, 2 * LANES)] = (active * ut[:, pl.ds(at, 2 * LANES)]).astype(BF16)
            if side == 0:
                sq[:, pl.ds(at, 2 * LANES)] = active * active
            else:
                both = (sq[:, pl.ds(at, 2 * LANES)] + active * active) * 0.5
                flat = both.T
                for j2 in range(2):
                    u32[pl.ds(jp * 2 + j2, ni, stride=jb), :] = flat[j2 * LANES : j2 * LANES + ni]
            for m in range(cc // 256):
                g = mm(w_ref[m * 256 : (m + 1) * 256, :], d[:, pl.ds(at, 2 * LANES)]).astype(BF16)
                for c in range(256 // CH):
                    for j2 in range(2):
                        to = pl.multiple_of(jp * 2 * CH + j2 * CH, CH)
                        ch = m * (256 // CH) + c
                        gx[pl.ds(to, CH), ch * LANES : (ch + 1) * LANES] = g[
                            c * CH : (c + 1) * CH, j2 * LANES : (j2 + 1) * LANES
                        ]
            return 0

        lax.fori_loop(0, jb // 2, second, 0)

        def fourth(cp, _):
            at = pl.multiple_of(cp * 2 * LANES, 2 * LANES)
            drt[side, :, pl.ds(at, 2 * LANES)] += mm(btt[...], gx[:, pl.ds(at, 2 * LANES)])
            return 0

        lax.fori_loop(0, CH // 2, fourth, 0)

        def fifth(m, _):
            at = pl.multiple_of(m * 256, 256)
            dct[1 - side, pl.ds(pl.multiple_of(base + at, 256), 256), :] = (
                mm(gx[pl.ds(at, 256), :], rx[side]) * scale
            ).astype(BF16)
            return 0

        lax.fori_loop(0, jb * CH // 256, fifth, 0)

        target = dw_ref if side == 0 else dw_m

        def sixth(m, _):
            at = pl.multiple_of(m * 256, 256)
            target[pl.ds(at, 256), :] += mm_nt(x[pl.ds(at, 256), :], d[...])
            return 0

        lax.fori_loop(0, cc // 256, sixth, 0)
        dw_ref[cc : cc + 8, :] += mm_nt(jnp.ones((8, jb * LANES), BF16), d[...])

    pair_ref[...] = u32[...].reshape(ni, jb, pairs).astype(BF16)

    @pl.when(step == last)
    def _():
        for side in range(2):

            def unpack(c, _):
                at = pl.multiple_of(c * LANES, LANES)
                wide[pl.ds(c, ni, stride=CH), :] = drt[side, :, pl.ds(at, LANES)].T[:ni] * scale
                return 0

            lax.fori_loop(0, CH, unpack, 0)
            for k in range(ndev):
                drows_ref[k, side] = wide[pl.ds(k * part, part), :].astype(BF16)
            for k in range(nparts):
                dcols_ref[k, side] = dct[side, pl.ds(k * part, part), :]

        def merge(c, _):
            at = pl.multiple_of(c * CH, CH)
            dw_ref[pl.ds(at, CH), :] += dw_m[pl.ds(c, CH, stride=CH), :]
            return 0

        lax.fori_loop(0, CH, merge, 0)


def tile(rows, cols, weight, bias, upstream):
    ni, nj, pairs = upstream.shape
    jb = 16
    cc = CH * CH
    mirrored = weight.reshape(CH, CH, pairs).transpose(1, 0, 2).reshape(cc, pairs)
    whole = pl.BlockSpec(memory_space=pltpu.VMEM)
    fixed = lambda shape: pl.BlockSpec(shape, lambda g: (0,) * len(shape))
    return pl.pallas_call(
        functools.partial(tile_kernel, jb, ni, nj),
        grid=(nj // jb,),
        in_specs=[whole] * 7 + [pl.BlockSpec((ni, jb, pairs), lambda g: (0, g, 0))],
        out_specs=[
            pl.BlockSpec((ni, jb, pairs), lambda g: (0, g, 0)),
            fixed(rows.shape),
            fixed(cols.shape),
            fixed((cc + 8, pairs)),
        ],
        out_shape=[
            jax.ShapeDtypeStruct((ni, nj, pairs), BF16),
            jax.ShapeDtypeStruct(rows.shape, BF16),
            jax.ShapeDtypeStruct(cols.shape, BF16),
            jax.ShapeDtypeStruct((cc + 8, pairs), F32),
        ],
        scratch_shapes=[
            pltpu.VMEM((2, SEQS, CH * LANES), BF16),
            pltpu.VMEM((2, CH * LANES, SEQS), BF16),
            pltpu.VMEM((2, nj * CH, SEQS), BF16),
            pltpu.VMEM((ni * CH, SEQS), F32),
            pltpu.VMEM((cc, jb * LANES), BF16),
            pltpu.VMEM((jb * CH, CH * LANES), BF16),
            pltpu.VMEM((pairs, jb * LANES), BF16),
            pltpu.VMEM((pairs, jb * LANES), F32),
            pltpu.VMEM((ni * jb, pairs), F32),
            pltpu.VMEM((pairs, jb * LANES), F32),
            pltpu.VMEM((2, SEQS, CH * LANES), F32),
            pltpu.VMEM((cc, pairs), F32),
            pltpu.VMEM((2, nj * CH, SEQS), BF16),
            pltpu.VMEM((SEQS, jb * CH), BF16),
        ],
        compiler_params=pltpu.CompilerParams(
            dimension_semantics=("arbitrary",), vmem_limit_bytes=50 * 1024 * 1024
        ),
    )(rows, cols, weight, mirrored, weight.T, mirrored.T, bias.reshape(pairs, 1), upstream)


def local(left_features, right_features, weight, bias, upstream):
    row_count = lax.axis_size("row")
    col_count = lax.axis_size("col")
    ratio = col_count // row_count
    col_index = lax.axis_index("col")
    own = left_features.shape[0]
    portion = col_index % ratio
    owner = col_index // ratio
    mine = jnp.stack([left_features, right_features]).reshape(2, own, SEQS, CH)
    mine = mine.transpose(0, 1, 3, 2).reshape(2, own * CH, SEQS)
    rows = lax.all_gather(mine, "col", axis=0)
    piece = lax.dynamic_slice_in_dim(rows, portion * row_count, row_count, 0)
    recv = lax.all_to_all(piece, "row", split_axis=0, concat_axis=0, tiled=True)
    part = lax.dynamic_index_in_dim(recv, owner, 0, keepdims=False)
    cols = lax.all_gather(part, "row", axis=0)
    pair_out, d_rows, d_cols, d_weight = tile(rows, cols, weight, bias, upstream)
    total = lax.psum(d_weight, ("row", "col"))
    from_col = lax.all_to_all(d_cols, "row", split_axis=0, concat_axis=0, tiled=True)
    col_sum = jnp.sum(from_col.astype(F32), axis=0).astype(BF16)
    moves = [
        (r * col_count + q, q * row_count + r) for r in range(row_count) for q in range(col_count)
    ]
    col_sum = lax.ppermute(col_sum, ("row", "col"), moves)
    from_row = lax.all_to_all(d_rows, "col", split_axis=0, concat_axis=0, tiled=True)
    grads = jnp.sum(from_row.astype(F32), axis=0) + col_sum.astype(F32)
    grads = grads.astype(BF16).reshape(2, own, CH, SEQS).transpose(0, 1, 3, 2)
    grads = grads.reshape(2, own, SEQS * CH)
    cc = CH * CH
    return pair_out, grads[0], grads[1], total[:cc], total[cc]


def solution(mesh):
    placed = (P(("row", "col"), None), P(("row", "col"), None), P(), P(), P("row", "col", None))
    return jax.shard_map(
        local,
        mesh=mesh,
        in_specs=placed,
        out_specs=(
            P("row", "col", None),
            P(("row", "col"), None),
            P(("row", "col"), None),
            P(),
            P(),
        ),
        check_vma=False,
    )
```

```python
import functools

import jax
import jax.numpy as jnp
from jax import lax
from jax.experimental import pallas as pl
from jax.experimental.pallas import tpu as pltpu
from jax.sharding import PartitionSpec as P

CH = 32
SEQS = 128
LANES = 128
F32 = jnp.float32
BF16 = jnp.bfloat16


def mm(a, b):
    return lax.dot_general(a, b, (((1,), (0,)), ((), ())), preferred_element_type=F32)


def mm_nt(a, b):
    return lax.dot_general(a, b, (((1,), (1,)), ((), ())), preferred_element_type=F32)


def tile_kernel(
    jb, ni, nj,
    rows_ref, cols_ref, wd_ref, wm_ref, wdt_ref, wmt_ref, bias_ref, up_ref,
    pair_ref, drows_ref, dcols_ref, dw_ref,
    rt, rx, bt, wide, x, gx, d, sq, u32, ut, drt, dw_m, dct, btt,
):
    step = pl.program_id(0)
    last = pl.num_programs(0) - 1
    pairs = wd_ref.shape[1]
    cc = CH * CH
    scale = 1.0 / SEQS
    ndev, _, part, _ = rows_ref.shape
    nparts = cols_ref.shape[0]
    pad = LANES - ni

    @pl.when(step == 0)
    def _():
        for side in range(2):
            for k in range(ndev):
                wide[pl.ds(k * part, part), :] = rows_ref[k, side].astype(F32)
            for k in range(nparts):
                bt[side, pl.ds(k * part, part), :] = cols_ref[k, side]

            def prep(c, _):
                block = wide[pl.ds(c, ni, stride=CH), :]
                if pad:
                    block = jnp.concatenate([block, jnp.zeros((pad, SEQS), F32)], axis=0)
                at = pl.multiple_of(c * LANES, LANES)
                rx[side, pl.ds(at, LANES), :] = block.astype(BF16)
                rt[side, :, pl.ds(at, LANES)] = block.T.astype(BF16)
                return 0

            lax.fori_loop(0, CH, prep, 0)
        drt[...] = jnp.zeros_like(drt)
        dw_ref[...] = jnp.zeros_like(dw_ref)
        dw_m[...] = jnp.zeros_like(dw_m)

    u32[...] = up_ref[...].astype(F32).reshape(ni * jb, pairs)
    for j in range(jb):
        block = u32[pl.ds(j, ni, stride=jb), :]
        if pad:
            block = jnp.concatenate([block, jnp.zeros((pad, pairs), F32)], axis=0)
        ut[:, j * LANES : (j + 1) * LANES] = block.T

    for side in range(2):
        w_ref, wt_ref = (wd_ref, wdt_ref) if side == 0 else (wm_ref, wmt_ref)
        base = pl.multiple_of(step * (jb * CH), jb * CH)
        bt_blk = bt[1 - side, pl.ds(base, jb * CH), :]
        btt[...] = bt_blk.astype(F32).T.astype(BF16)

        def first(cp, _):
            at = pl.multiple_of(cp * 2 * LANES, 2 * LANES)
            r = mm(bt[1 - side, pl.ds(base, jb * CH), :], rt[side, :, pl.ds(at, 2 * LANES)])
            r = (r * scale).astype(BF16)
            for c2 in range(2):
                to = pl.multiple_of(cp * 2 * CH + c2 * CH, CH)
                for j in range(jb):
                    x[pl.ds(to, CH), j * LANES : (j + 1) * LANES] = r[
                        j * CH : (j + 1) * CH, c2 * LANES : (c2 + 1) * LANES
                    ]
            return 0

        lax.fori_loop(0, CH // 2, first, 0)

        def second(jp, _):
            at = pl.multiple_of(jp * 2 * LANES, 2 * LANES)
            pre = mm(wt_ref[...], x[:, pl.ds(at, 2 * LANES)]) + bias_ref[...]
            active = jnp.maximum(pre, 0.0)
            d[:, pl.ds(at, 2 * LANES)] = (active * ut[:, pl.ds(at, 2 * LANES)]).astype(BF16)
            if side == 0:
                sq[:, pl.ds(at, 2 * LANES)] = active * active
            else:
                both = (sq[:, pl.ds(at, 2 * LANES)] + active * active) * 0.5
                flat = both.T
                for j2 in range(2):
                    u32[pl.ds(jp * 2 + j2, ni, stride=jb), :] = flat[j2 * LANES : j2 * LANES + ni]
            for m in range(cc // 256):
                g = mm(w_ref[m * 256 : (m + 1) * 256, :], d[:, pl.ds(at, 2 * LANES)]).astype(BF16)
                for c in range(256 // CH):
                    for j2 in range(2):
                        to = pl.multiple_of(jp * 2 * CH + j2 * CH, CH)
                        ch = m * (256 // CH) + c
                        gx[pl.ds(to, CH), ch * LANES : (ch + 1) * LANES] = g[
                            c * CH : (c + 1) * CH, j2 * LANES : (j2 + 1) * LANES
                        ]
            return 0

        lax.fori_loop(0, jb // 2, second, 0)

        def fourth(cp, _):
            at = pl.multiple_of(cp * 2 * LANES, 2 * LANES)
            drt[side, :, pl.ds(at, 2 * LANES)] += mm(btt[...], gx[:, pl.ds(at, 2 * LANES)])
            return 0

        lax.fori_loop(0, CH // 2, fourth, 0)

        def fifth(m, _):
            at = pl.multiple_of(m * 256, 256)
            dct[1 - side, pl.ds(pl.multiple_of(base + at, 256), 256), :] = (
                mm(gx[pl.ds(at, 256), :], rx[side]) * scale
            ).astype(BF16)
            return 0

        lax.fori_loop(0, jb * CH // 256, fifth, 0)

        target = dw_ref if side == 0 else dw_m

        def sixth(m, _):
            at = pl.multiple_of(m * 256, 256)
            target[pl.ds(at, 256), :] += mm_nt(x[pl.ds(at, 256), :], d[...])
            return 0

        lax.fori_loop(0, cc // 256, sixth, 0)
        dw_ref[cc : cc + 8, :] += mm_nt(jnp.ones((8, jb * LANES), BF16), d[...])

    pair_ref[...] = u32[...].reshape(ni, jb, pairs).astype(BF16)

    @pl.when(step == last)
    def _():
        for side in range(2):

            def unpack(c, _):
                at = pl.multiple_of(c * LANES, LANES)
                wide[pl.ds(c, ni, stride=CH), :] = drt[side, :, pl.ds(at, LANES)].T[:ni] * scale
                return 0

            lax.fori_loop(0, CH, unpack, 0)
            for k in range(ndev):
                drows_ref[k, side] = wide[pl.ds(k * part, part), :].astype(BF16)
            for k in range(nparts):
                dcols_ref[k, side] = dct[side, pl.ds(k * part, part), :]

        def merge(c, _):
            at = pl.multiple_of(c * CH, CH)
            dw_ref[pl.ds(at, CH), :] += dw_m[pl.ds(c, CH, stride=CH), :]
            return 0

        lax.fori_loop(0, CH, merge, 0)


def tile(rows, cols, weight, bias, upstream):
    ni, nj, pairs = upstream.shape
    jb = 16
    cc = CH * CH
    mirrored = weight.reshape(CH, CH, pairs).transpose(1, 0, 2).reshape(cc, pairs)
    whole = pl.BlockSpec(memory_space=pltpu.VMEM)
    fixed = lambda shape: pl.BlockSpec(shape, lambda g: (0,) * len(shape))
    return pl.pallas_call(
        functools.partial(tile_kernel, jb, ni, nj),
        grid=(nj // jb,),
        in_specs=[whole] * 7 + [pl.BlockSpec((ni, jb, pairs), lambda g: (0, g, 0))],
        out_specs=[
            pl.BlockSpec((ni, jb, pairs), lambda g: (0, g, 0)),
            fixed(rows.shape),
            fixed(cols.shape),
            fixed((cc + 8, pairs)),
        ],
        out_shape=[
            jax.ShapeDtypeStruct((ni, nj, pairs), BF16),
            jax.ShapeDtypeStruct(rows.shape, BF16),
            jax.ShapeDtypeStruct(cols.shape, BF16),
            jax.ShapeDtypeStruct((cc + 8, pairs), F32),
        ],
        scratch_shapes=[
            pltpu.VMEM((2, SEQS, CH * LANES), BF16),
            pltpu.VMEM((2, CH * LANES, SEQS), BF16),
            pltpu.VMEM((2, nj * CH, SEQS), BF16),
            pltpu.VMEM((ni * CH, SEQS), F32),
            pltpu.VMEM((cc, jb * LANES), BF16),
            pltpu.VMEM((jb * CH, CH * LANES), BF16),
            pltpu.VMEM((pairs, jb * LANES), BF16),
            pltpu.VMEM((pairs, jb * LANES), F32),
            pltpu.VMEM((ni * jb, pairs), F32),
            pltpu.VMEM((pairs, jb * LANES), F32),
            pltpu.VMEM((2, SEQS, CH * LANES), F32),
            pltpu.VMEM((cc, pairs), F32),
            pltpu.VMEM((2, nj * CH, SEQS), BF16),
            pltpu.VMEM((SEQS, jb * CH), BF16),
        ],
        compiler_params=pltpu.CompilerParams(
            dimension_semantics=("arbitrary",), vmem_limit_bytes=50 * 1024 * 1024
        ),
    )(rows, cols, weight, mirrored, weight.T, mirrored.T, bias.reshape(pairs, 1), upstream)


def local(left_features, right_features, weight, bias, upstream):
    row_count = lax.axis_size("row")
    col_count = lax.axis_size("col")
    ratio = col_count // row_count
    col_index = lax.axis_index("col")
    own = left_features.shape[0]
    portion = col_index % ratio
    owner = col_index // ratio
    mine = jnp.stack([left_features, right_features]).reshape(2, own, SEQS, CH)
    mine = mine.transpose(0, 1, 3, 2).reshape(2, own * CH, SEQS)
    rows = lax.all_gather(mine, "col", axis=0)
    piece = lax.dynamic_slice_in_dim(rows, portion * row_count, row_count, 0)
    recv = lax.all_to_all(piece, "row", split_axis=0, concat_axis=0, tiled=True)
    part = lax.dynamic_index_in_dim(recv, owner, 0, keepdims=False)
    cols = lax.all_gather(part, "row", axis=0)
    pair_out, d_rows, d_cols, d_weight = tile(rows, cols, weight, bias, upstream)
    cc, pairs = weight.shape
    joint = d_weight.astype(BF16)
    send = jnp.concatenate(
        [
            d_rows.reshape(col_count, 2 * own * CH, SEQS),
            joint[:cc].reshape(col_count, cc // col_count, pairs),
            jnp.broadcast_to(joint[cc:][None], (col_count, 8, pairs)),
        ],
        axis=1,
    )
    from_row = lax.all_to_all(send, "col", split_axis=0, concat_axis=0, tiled=True)
    row_sum = jnp.sum(from_row.astype(F32), axis=0)
    size = 2 * own * CH
    joint = row_sum[size:].astype(BF16)
    deep = cc // col_count
    send = jnp.concatenate(
        [
            d_cols.reshape(row_count, size, SEQS),
            joint[:deep].reshape(row_count, deep // row_count, pairs),
            jnp.broadcast_to(joint[deep:][None], (row_count, 8, pairs)),
        ],
        axis=1,
    )
    from_col = lax.all_to_all(send, "row", split_axis=0, concat_axis=0, tiled=True)
    col_sum = jnp.sum(from_col.astype(F32), axis=0)
    chunk = col_sum[size : size + deep // row_count]
    grad_bias = col_sum[size + deep // row_count]
    grad_weight = lax.all_gather(chunk, ("col", "row"), axis=0, tiled=True)
    moves = [
        (r * col_count + q, q * row_count + r) for r in range(row_count) for q in range(col_count)
    ]
    col_sum = lax.ppermute(col_sum[:size].astype(BF16), ("row", "col"), moves)
    grads = row_sum[:size] + col_sum.astype(F32)
    grads = grads.astype(BF16).reshape(2, own, CH, SEQS).transpose(0, 1, 3, 2)
    grads = grads.reshape(2, own, SEQS * CH)
    return pair_out, grads[0], grads[1], grad_weight, grad_bias


def solution(mesh):
    placed = (P(("row", "col"), None), P(("row", "col"), None), P(), P(), P("row", "col", None))
    return jax.shard_map(
        local,
        mesh=mesh,
        in_specs=placed,
        out_specs=(
            P("row", "col", None),
            P(("row", "col"), None),
            P(("row", "col"), None),
            P(),
            P(),
        ),
        check_vma=False,
    )
```

```python
import functools

import jax
import jax.numpy as jnp
from jax import lax
from jax.experimental import pallas as pl
from jax.experimental.pallas import tpu as pltpu
from jax.sharding import PartitionSpec as P

CH = 32
SEQS = 128
LANES = 128
F32 = jnp.float32
BF16 = jnp.bfloat16


def mm(a, b):
    return lax.dot_general(a, b, (((1,), (0,)), ((), ())), preferred_element_type=F32)


def mm_nt(a, b):
    return lax.dot_general(a, b, (((1,), (1,)), ((), ())), preferred_element_type=F32)


def tile_kernel(
    jb, ni, nj,
    rows_ref, cols_ref, wd_ref, wm_ref, wdt_ref, wmt_ref, bias_ref, up_ref,
    pair_ref, drows_ref, dcols_ref, dw_ref,
    rt, rx, bt, wide, x, gx, d, sq, u32, ut, drt, dw_m, dct, btt,
):
    step = pl.program_id(0)
    last = pl.num_programs(0) - 1
    pairs = wd_ref.shape[1]
    cc = CH * CH
    scale = 1.0 / SEQS
    ndev, _, part, _ = rows_ref.shape
    nparts = cols_ref.shape[0]
    pad = LANES - ni

    @pl.when(step == 0)
    def _():
        for side in range(2):
            for k in range(ndev):
                wide[pl.ds(k * part, part), :] = rows_ref[k, side].astype(F32)
            for k in range(nparts):
                bt[side, pl.ds(k * part, part), :] = cols_ref[k, side]

            def prep(c, _):
                block = wide[pl.ds(c, ni, stride=CH), :]
                if pad:
                    block = jnp.concatenate([block, jnp.zeros((pad, SEQS), F32)], axis=0)
                at = pl.multiple_of(c * LANES, LANES)
                rx[side, pl.ds(at, LANES), :] = block.astype(BF16)
                rt[side, :, pl.ds(at, LANES)] = block.T.astype(BF16)
                return 0

            lax.fori_loop(0, CH, prep, 0)
        drt[...] = jnp.zeros_like(drt)
        dw_ref[...] = jnp.zeros_like(dw_ref)
        dw_m[...] = jnp.zeros_like(dw_m)

    u32[...] = up_ref[...].astype(F32).reshape(ni * jb, pairs)
    for j in range(jb):
        block = u32[pl.ds(j, ni, stride=jb), :]
        if pad:
            block = jnp.concatenate([block, jnp.zeros((pad, pairs), F32)], axis=0)
        ut[:, j * LANES : (j + 1) * LANES] = block.T

    for side in range(2):
        w_ref, wt_ref = (wd_ref, wdt_ref) if side == 0 else (wm_ref, wmt_ref)
        base = pl.multiple_of(step * (jb * CH), jb * CH)
        bt_blk = bt[1 - side, pl.ds(base, jb * CH), :]
        btt[...] = bt_blk.astype(F32).T.astype(BF16)

        def first(cp, _):
            at = pl.multiple_of(cp * 2 * LANES, 2 * LANES)
            r = mm(bt[1 - side, pl.ds(base, jb * CH), :], rt[side, :, pl.ds(at, 2 * LANES)])
            r = (r * scale).astype(BF16)
            for c2 in range(2):
                to = pl.multiple_of(cp * 2 * CH + c2 * CH, CH)
                for j in range(jb):
                    x[pl.ds(to, CH), j * LANES : (j + 1) * LANES] = r[
                        j * CH : (j + 1) * CH, c2 * LANES : (c2 + 1) * LANES
                    ]
            return 0

        lax.fori_loop(0, CH // 2, first, 0)

        def second(jp, _):
            at = pl.multiple_of(jp * 2 * LANES, 2 * LANES)
            pre = mm(wt_ref[...], x[:, pl.ds(at, 2 * LANES)]) + bias_ref[...]
            active = jnp.maximum(pre, 0.0)
            d[:, pl.ds(at, 2 * LANES)] = (active * ut[:, pl.ds(at, 2 * LANES)]).astype(BF16)
            if side == 0:
                sq[:, pl.ds(at, 2 * LANES)] = active * active
            else:
                both = (sq[:, pl.ds(at, 2 * LANES)] + active * active) * 0.5
                flat = both.T
                for j2 in range(2):
                    u32[pl.ds(jp * 2 + j2, ni, stride=jb), :] = flat[j2 * LANES : j2 * LANES + ni]
            for m in range(cc // 256):
                g = mm(w_ref[m * 256 : (m + 1) * 256, :], d[:, pl.ds(at, 2 * LANES)]).astype(BF16)
                for c in range(256 // CH):
                    for j2 in range(2):
                        to = pl.multiple_of(jp * 2 * CH + j2 * CH, CH)
                        ch = m * (256 // CH) + c
                        gx[pl.ds(to, CH), ch * LANES : (ch + 1) * LANES] = g[
                            c * CH : (c + 1) * CH, j2 * LANES : (j2 + 1) * LANES
                        ]
            return 0

        lax.fori_loop(0, jb // 2, second, 0)

        def fourth(cp, _):
            at = pl.multiple_of(cp * 2 * LANES, 2 * LANES)
            drt[side, :, pl.ds(at, 2 * LANES)] += mm(btt[...], gx[:, pl.ds(at, 2 * LANES)])
            return 0

        lax.fori_loop(0, CH // 2, fourth, 0)

        def fifth(m, _):
            at = pl.multiple_of(m * 256, 256)
            dct[1 - side, pl.ds(pl.multiple_of(base + at, 256), 256), :] = (
                mm(gx[pl.ds(at, 256), :], rx[side]) * scale
            ).astype(BF16)
            return 0

        lax.fori_loop(0, jb * CH // 256, fifth, 0)

        target = dw_ref if side == 0 else dw_m

        def sixth(m, _):
            at = pl.multiple_of(m * 256, 256)
            target[pl.ds(at, 256), :] += mm_nt(x[pl.ds(at, 256), :], d[...])
            return 0

        lax.fori_loop(0, cc // 256, sixth, 0)
        dw_ref[cc : cc + 8, :] += mm_nt(jnp.ones((8, jb * LANES), BF16), d[...])

    pair_ref[...] = u32[...].reshape(ni, jb, pairs).astype(BF16)

    @pl.when(step == last)
    def _():
        for side in range(2):

            def unpack(c, _):
                at = pl.multiple_of(c * LANES, LANES)
                wide[pl.ds(c, ni, stride=CH), :] = drt[side, :, pl.ds(at, LANES)].T[:ni] * scale
                return 0

            lax.fori_loop(0, CH, unpack, 0)
            for k in range(ndev):
                drows_ref[k, side] = wide[pl.ds(k * part, part), :].astype(BF16)
            for k in range(nparts):
                dcols_ref[k, side] = dct[side, pl.ds(k * part, part), :]

        def merge(c, _):
            at = pl.multiple_of(c * CH, CH)
            dw_ref[pl.ds(at, CH), :] += dw_m[pl.ds(c, CH, stride=CH), :]
            return 0

        lax.fori_loop(0, CH, merge, 0)


def tile(rows, cols, weight, bias, upstream):
    ni, nj, pairs = upstream.shape
    jb = 16
    cc = CH * CH
    mirrored = weight.reshape(CH, CH, pairs).transpose(1, 0, 2).reshape(cc, pairs)
    whole = pl.BlockSpec(memory_space=pltpu.VMEM)
    fixed = lambda shape: pl.BlockSpec(shape, lambda g: (0,) * len(shape))
    return pl.pallas_call(
        functools.partial(tile_kernel, jb, ni, nj),
        grid=(nj // jb,),
        in_specs=[whole] * 7 + [pl.BlockSpec((ni, jb, pairs), lambda g: (0, g, 0))],
        out_specs=[
            pl.BlockSpec((ni, jb, pairs), lambda g: (0, g, 0)),
            fixed(rows.shape),
            fixed(cols.shape),
            fixed((cc + 8, pairs)),
        ],
        out_shape=[
            jax.ShapeDtypeStruct((ni, nj, pairs), BF16),
            jax.ShapeDtypeStruct(rows.shape, BF16),
            jax.ShapeDtypeStruct(cols.shape, BF16),
            jax.ShapeDtypeStruct((cc + 8, pairs), F32),
        ],
        scratch_shapes=[
            pltpu.VMEM((2, SEQS, CH * LANES), BF16),
            pltpu.VMEM((2, CH * LANES, SEQS), BF16),
            pltpu.VMEM((2, nj * CH, SEQS), BF16),
            pltpu.VMEM((ni * CH, SEQS), F32),
            pltpu.VMEM((cc, jb * LANES), BF16),
            pltpu.VMEM((jb * CH, CH * LANES), BF16),
            pltpu.VMEM((pairs, jb * LANES), BF16),
            pltpu.VMEM((pairs, jb * LANES), F32),
            pltpu.VMEM((ni * jb, pairs), F32),
            pltpu.VMEM((pairs, jb * LANES), F32),
            pltpu.VMEM((2, SEQS, CH * LANES), F32),
            pltpu.VMEM((cc, pairs), F32),
            pltpu.VMEM((2, nj * CH, SEQS), BF16),
            pltpu.VMEM((SEQS, jb * CH), BF16),
        ],
        compiler_params=pltpu.CompilerParams(
            dimension_semantics=("arbitrary",), vmem_limit_bytes=50 * 1024 * 1024
        ),
    )(rows, cols, weight, mirrored, weight.T, mirrored.T, bias.reshape(pairs, 1), upstream)


def local(left_features, right_features, weight, bias, upstream):
    row_count = lax.axis_size("row")
    col_count = lax.axis_size("col")
    ratio = col_count // row_count
    col_index = lax.axis_index("col")
    own = left_features.shape[0]
    portion = col_index % ratio
    owner = col_index // ratio
    mine = jnp.stack([left_features, right_features]).reshape(2, own, SEQS, CH)
    mine = mine.transpose(0, 1, 3, 2).reshape(2, own * CH, SEQS)
    rows = lax.all_gather(mine, "col", axis=0)
    piece = lax.dynamic_slice_in_dim(rows, portion * row_count, row_count, 0)
    recv = lax.all_to_all(piece, "row", split_axis=0, concat_axis=0, tiled=True)
    part = lax.dynamic_index_in_dim(recv, owner, 0, keepdims=False)
    cols = lax.all_gather(part, "row", axis=0)
    pair_out, d_rows, d_cols, d_weight = tile(rows, cols, weight, bias, upstream)
    cc, pairs = weight.shape
    joint = d_weight.astype(BF16)
    send = jnp.concatenate(
        [
            d_rows.reshape(col_count, 2 * own * CH, SEQS),
            joint[:cc].reshape(col_count, cc // col_count, pairs),
            jnp.broadcast_to(joint[cc:][None], (col_count, 8, pairs)),
        ],
        axis=1,
    )
    from_row = lax.all_to_all(send, "col", split_axis=0, concat_axis=0, tiled=True)
    row_sum = jnp.sum(from_row.astype(F32), axis=0)
    size = 2 * own * CH
    joint = row_sum[size:].astype(BF16)
    deep = cc // col_count
    send = jnp.concatenate(
        [
            d_cols.reshape(row_count, size, SEQS),
            joint[:deep].reshape(row_count, deep // row_count, pairs),
            jnp.broadcast_to(joint[deep:][None], (row_count, 8, pairs)),
        ],
        axis=1,
    )
    from_col = lax.all_to_all(send, "row", split_axis=0, concat_axis=0, tiled=True)
    col_sum = jnp.sum(from_col.astype(F32), axis=0)
    chunk = col_sum[size : size + deep // row_count]
    grad_bias = col_sum[size + deep // row_count]
    grad_weight = lax.all_gather(chunk, "row", axis=0, tiled=True)
    grad_weight = lax.all_gather(grad_weight, "col", axis=0, tiled=True)
    moves = [
        (r * col_count + q, q * row_count + r) for r in range(row_count) for q in range(col_count)
    ]
    col_sum = lax.ppermute(col_sum[:size].astype(BF16), ("row", "col"), moves)
    grads = row_sum[:size] + col_sum.astype(F32)
    grads = grads.astype(BF16).reshape(2, own, CH, SEQS).transpose(0, 1, 3, 2)
    grads = grads.reshape(2, own, SEQS * CH)
    return pair_out, grads[0], grads[1], grad_weight, grad_bias


def solution(mesh):
    placed = (P(("row", "col"), None), P(("row", "col"), None), P(), P(), P("row", "col", None))
    return jax.shard_map(
        local,
        mesh=mesh,
        in_specs=placed,
        out_specs=(
            P("row", "col", None),
            P(("row", "col"), None),
            P(("row", "col"), None),
            P(),
            P(),
        ),
        check_vma=False,
    )
```

```python
import functools

import jax
import jax.numpy as jnp
from jax import lax
from jax.experimental import pallas as pl
from jax.experimental.pallas import tpu as pltpu
from jax.sharding import PartitionSpec as P

CH = 32
SEQS = 128
LANES = 128
F32 = jnp.float32
BF16 = jnp.bfloat16


def mm(a, b):
    return lax.dot_general(a, b, (((1,), (0,)), ((), ())), preferred_element_type=F32)


def mm_nt(a, b):
    return lax.dot_general(a, b, (((1,), (1,)), ((), ())), preferred_element_type=F32)


def tile_kernel(
    jb, ni, nj,
    rows_ref, cols_ref, wd_ref, wm_ref, wdt_ref, wmt_ref, bias_ref, up_ref,
    pair_ref, drows_ref, dcols_ref, dw_ref,
    rt, rx, bt, wide, x, gx, d, sq, u32, ut, drt, dw_m, dct, btt,
):
    step = pl.program_id(0)
    last = pl.num_programs(0) - 1
    pairs = wd_ref.shape[1]
    cc = CH * CH
    scale = 1.0 / SEQS
    ndev, _, part, _ = rows_ref.shape
    nparts = cols_ref.shape[0]
    pad = LANES - ni

    @pl.when(step == 0)
    def _():
        for side in range(2):
            for k in range(ndev):
                wide[pl.ds(k * part, part), :] = rows_ref[k, side].astype(F32)
            for k in range(nparts):
                bt[side, pl.ds(k * part, part), :] = cols_ref[k, side]

            def prep(c, _):
                block = wide[pl.ds(c, ni, stride=CH), :]
                if pad:
                    block = jnp.concatenate([block, jnp.zeros((pad, SEQS), F32)], axis=0)
                at = pl.multiple_of(c * LANES, LANES)
                rx[side, pl.ds(at, LANES), :] = block.astype(BF16)
                rt[side, :, pl.ds(at, LANES)] = block.T.astype(BF16)
                return 0

            lax.fori_loop(0, CH, prep, 0)
        drt[...] = jnp.zeros_like(drt)
        dw_ref[...] = jnp.zeros_like(dw_ref)
        dw_m[...] = jnp.zeros_like(dw_m)

    u32[...] = up_ref[...].astype(F32).reshape(ni * jb, pairs)
    for j in range(jb):
        block = u32[pl.ds(j, ni, stride=jb), :]
        if pad:
            block = jnp.concatenate([block, jnp.zeros((pad, pairs), F32)], axis=0)
        ut[:, j * LANES : (j + 1) * LANES] = block.T

    for side in range(2):
        w_ref, wt_ref = (wd_ref, wdt_ref) if side == 0 else (wm_ref, wmt_ref)
        base = pl.multiple_of(step * (jb * CH), jb * CH)
        bt_blk = bt[1 - side, pl.ds(base, jb * CH), :]
        btt[...] = bt_blk.astype(F32).T.astype(BF16)

        def first(cp, _):
            at = pl.multiple_of(cp * 2 * LANES, 2 * LANES)
            r = mm(bt[1 - side, pl.ds(base, jb * CH), :], rt[side, :, pl.ds(at, 2 * LANES)])
            r = (r * scale).astype(BF16)
            for c2 in range(2):
                to = pl.multiple_of(cp * 2 * CH + c2 * CH, CH)
                for j in range(jb):
                    x[pl.ds(to, CH), j * LANES : (j + 1) * LANES] = r[
                        j * CH : (j + 1) * CH, c2 * LANES : (c2 + 1) * LANES
                    ]
            return 0

        lax.fori_loop(0, CH // 2, first, 0)

        def second(jp, _):
            at = pl.multiple_of(jp * 2 * LANES, 2 * LANES)
            pre = mm(wt_ref[...], x[:, pl.ds(at, 2 * LANES)]) + bias_ref[...]
            active = jnp.maximum(pre, 0.0)
            d[:, pl.ds(at, 2 * LANES)] = (active * ut[:, pl.ds(at, 2 * LANES)]).astype(BF16)
            if side == 0:
                sq[:, pl.ds(at, 2 * LANES)] = active * active
            else:
                both = (sq[:, pl.ds(at, 2 * LANES)] + active * active) * 0.5
                flat = both.T
                for j2 in range(2):
                    u32[pl.ds(jp * 2 + j2, ni, stride=jb), :] = flat[j2 * LANES : j2 * LANES + ni]
            for m in range(cc // 256):
                g = mm(w_ref[m * 256 : (m + 1) * 256, :], d[:, pl.ds(at, 2 * LANES)]).astype(BF16)
                for c in range(256 // CH):
                    for j2 in range(2):
                        to = pl.multiple_of(jp * 2 * CH + j2 * CH, CH)
                        ch = m * (256 // CH) + c
                        gx[pl.ds(to, CH), ch * LANES : (ch + 1) * LANES] = g[
                            c * CH : (c + 1) * CH, j2 * LANES : (j2 + 1) * LANES
                        ]
            return 0

        lax.fori_loop(0, jb // 2, second, 0)

        def fourth(cp, _):
            at = pl.multiple_of(cp * 2 * LANES, 2 * LANES)
            drt[side, :, pl.ds(at, 2 * LANES)] += mm(btt[...], gx[:, pl.ds(at, 2 * LANES)])
            return 0

        lax.fori_loop(0, CH // 2, fourth, 0)

        def fifth(m, _):
            at = pl.multiple_of(m * 256, 256)
            dct[1 - side, pl.ds(pl.multiple_of(base + at, 256), 256), :] = (
                mm(gx[pl.ds(at, 256), :], rx[side]) * scale
            ).astype(BF16)
            return 0

        lax.fori_loop(0, jb * CH // 256, fifth, 0)

        target = dw_ref if side == 0 else dw_m

        def sixth(m, _):
            at = pl.multiple_of(m * 256, 256)
            target[pl.ds(at, 256), :] += mm_nt(x[pl.ds(at, 256), :], d[...])
            return 0

        lax.fori_loop(0, cc // 256, sixth, 0)
        dw_ref[cc : cc + 8, :] += mm_nt(jnp.ones((8, jb * LANES), BF16), d[...])

    pair_ref[...] = u32[...].reshape(ni, jb, pairs).astype(BF16)

    @pl.when(step == last)
    def _():
        for side in range(2):

            def unpack(c, _):
                at = pl.multiple_of(c * LANES, LANES)
                wide[pl.ds(c, ni, stride=CH), :] = drt[side, :, pl.ds(at, LANES)].T[:ni] * scale
                return 0

            lax.fori_loop(0, CH, unpack, 0)
            for k in range(ndev):
                drows_ref[k, side] = wide[pl.ds(k * part, part), :].astype(BF16)
            for k in range(nparts):
                dcols_ref[k, side] = dct[side, pl.ds(k * part, part), :]

        def merge(c, _):
            at = pl.multiple_of(c * CH, CH)
            dw_ref[pl.ds(at, CH), :] += dw_m[pl.ds(c, CH, stride=CH), :]
            return 0

        lax.fori_loop(0, CH, merge, 0)


def tile(rows, cols, weight, bias, upstream):
    ni, nj, pairs = upstream.shape
    jb = 16
    cc = CH * CH
    mirrored = weight.reshape(CH, CH, pairs).transpose(1, 0, 2).reshape(cc, pairs)
    whole = pl.BlockSpec(memory_space=pltpu.VMEM)
    fixed = lambda shape: pl.BlockSpec(shape, lambda g: (0,) * len(shape))
    return pl.pallas_call(
        functools.partial(tile_kernel, jb, ni, nj),
        grid=(nj // jb,),
        in_specs=[whole] * 7 + [pl.BlockSpec((ni, jb, pairs), lambda g: (0, g, 0))],
        out_specs=[
            pl.BlockSpec((ni, jb, pairs), lambda g: (0, g, 0)),
            fixed(rows.shape),
            fixed(cols.shape),
            fixed((cc + 8, pairs)),
        ],
        out_shape=[
            jax.ShapeDtypeStruct((ni, nj, pairs), BF16),
            jax.ShapeDtypeStruct(rows.shape, BF16),
            jax.ShapeDtypeStruct(cols.shape, BF16),
            jax.ShapeDtypeStruct((cc + 8, pairs), F32),
        ],
        scratch_shapes=[
            pltpu.VMEM((2, SEQS, CH * LANES), BF16),
            pltpu.VMEM((2, CH * LANES, SEQS), BF16),
            pltpu.VMEM((2, nj * CH, SEQS), BF16),
            pltpu.VMEM((ni * CH, SEQS), F32),
            pltpu.VMEM((cc, jb * LANES), BF16),
            pltpu.VMEM((jb * CH, CH * LANES), BF16),
            pltpu.VMEM((pairs, jb * LANES), BF16),
            pltpu.VMEM((pairs, jb * LANES), F32),
            pltpu.VMEM((ni * jb, pairs), F32),
            pltpu.VMEM((pairs, jb * LANES), F32),
            pltpu.VMEM((2, SEQS, CH * LANES), F32),
            pltpu.VMEM((cc, pairs), F32),
            pltpu.VMEM((2, nj * CH, SEQS), BF16),
            pltpu.VMEM((SEQS, jb * CH), BF16),
        ],
        compiler_params=pltpu.CompilerParams(
            dimension_semantics=("arbitrary",), vmem_limit_bytes=50 * 1024 * 1024
        ),
    )(rows, cols, weight, mirrored, weight.T, mirrored.T, bias.reshape(pairs, 1), upstream)


def local(left_features, right_features, weight, bias, upstream):
    row_count = lax.axis_size("row")
    col_count = lax.axis_size("col")
    ratio = col_count // row_count
    col_index = lax.axis_index("col")
    own = left_features.shape[0]
    portion = col_index % ratio
    owner = col_index // ratio
    mine = jnp.stack([left_features, right_features]).reshape(2, own, SEQS, CH)
    mine = mine.transpose(0, 1, 3, 2).reshape(2, own * CH, SEQS)
    rows = lax.all_gather(mine, "col", axis=0)
    piece = lax.dynamic_slice_in_dim(rows, portion * row_count, row_count, 0)
    recv = lax.all_to_all(piece, "row", split_axis=0, concat_axis=0, tiled=True)
    part = lax.dynamic_index_in_dim(recv, owner, 0, keepdims=False)
    cols = lax.all_gather(part, "row", axis=0)
    pair_out, d_rows, d_cols, d_weight = tile(rows, cols, weight, bias, upstream)
    cc, pairs = weight.shape
    joint = d_weight.astype(BF16)
    send = jnp.concatenate(
        [
            joint[:cc].reshape(col_count, cc // col_count, pairs),
            jnp.broadcast_to(joint[cc:][None], (col_count, 8, pairs)),
        ],
        axis=1,
    )
    size = 2 * own * CH
    from_row = lax.all_to_all(d_rows, "col", split_axis=0, concat_axis=0, tiled=True)
    shared = lax.all_to_all(send, "col", split_axis=0, concat_axis=0, tiled=True)
    joint = jnp.sum(shared.astype(F32), axis=0).astype(BF16)
    deep = cc // col_count
    send = jnp.concatenate(
        [
            d_cols.reshape(row_count, size, SEQS),
            joint[:deep].reshape(row_count, deep // row_count, pairs),
            jnp.broadcast_to(joint[deep:][None], (row_count, 8, pairs)),
        ],
        axis=1,
    )
    from_col = lax.all_to_all(send, "row", split_axis=0, concat_axis=0, tiled=True)
    col_sum = jnp.sum(from_col.astype(F32), axis=0)
    chunk = col_sum[size : size + deep // row_count]
    grad_bias = col_sum[size + deep // row_count]
    grad_weight = lax.all_gather(chunk, "row", axis=0, tiled=True)
    grad_weight = lax.all_gather(grad_weight, "col", axis=0, tiled=True)
    moves = [
        (r * col_count + q, q * row_count + r) for r in range(row_count) for q in range(col_count)
    ]
    col_sum = lax.ppermute(col_sum[:size].astype(BF16), ("row", "col"), moves)
    row_sum = jnp.sum(from_row.astype(F32), axis=0).reshape(size, SEQS)
    grads = row_sum + col_sum.astype(F32)
    grads = grads.astype(BF16).reshape(2, own, CH, SEQS).transpose(0, 1, 3, 2)
    grads = grads.reshape(2, own, SEQS * CH)
    return pair_out, grads[0], grads[1], grad_weight, grad_bias


def solution(mesh):
    placed = (P(("row", "col"), None), P(("row", "col"), None), P(), P(), P("row", "col", None))
    return jax.shard_map(
        local,
        mesh=mesh,
        in_specs=placed,
        out_specs=(
            P("row", "col", None),
            P(("row", "col"), None),
            P(("row", "col"), None),
            P(),
            P(),
        ),
        check_vma=False,
    )
```
